32 devices in a mesh: groups: 2 (over y), map: 16 (over z, x, core).
Axes of the slice: x: 2, y: 2, z: 4, core: 2. Of those that a mesh axis runs over, the one named last changes fastest.
Arguments:
- amplitude_maps: bfloat16 [400, 512, 512], P('groups', 'map'), parts along dimension 0, may hold values from -6 to 6
- kept_blocks: int32 [512], P(('groups', 'map')), parts along dimension 0, may hold values from 0 to 2047, as said below
- block_owner: int32 [512, 1], P(('groups', 'map')), parts along dimension 0, may hold values from 0 to 15; in each aligned block of 16 rows (0 to 15, 16 to 31, ...) at most 2 rows name the same one
- observed: bfloat16 [8192], P(('groups', 'map')), parts along dimension 0, may hold values from -8 to 8
- error_scale: bfloat16 [8192], P(('groups', 'map')), parts along dimension 0, may hold values from 0.5 to 1.59375
- perturbation: bfloat16 [8192, 200], P(('groups', 'map')), parts along dimension 0, may hold values from -6 to 6
- model_slab: bfloat16 [200, 393216], P(None, ('groups', 'map')), parts along dimension 1, may hold values from -6 to 6
Outputs:
- updated_slab: bfloat16 [200, 393216], P(None, ('groups', 'map')), parts along dimension 1
- update_weights: float32 [400, 200], P('groups'), parts along dimension 0
- data_misfit: float32 [8192], P(('groups', 'map')), parts along dimension 0
The draws below stay inside these ranges and needn't reach their ends.
There are 2 independent parts, one for each index of `groups`. The reference program is written for one: setup_inputs(seed, part) draws one part's arguments, and reference() takes and returns one part's arrays. A program takes and returns all parts, laid end to end along the dimension named above; each array names one. Nothing has to cross between parts.
Inputs may be any that keep to these rules, and one draw needn't show every extreme that they name: `kept_blocks`: the 16 entries of one device are distinct numbers of that device's own 2048 blocks. `block_owner`: at most 2 of the 16 kept blocks of one device share an owner.
All inputs are finite; a program needn't handle non-finite values.
Results may differ from the reference program's by a relative error of at most 0.0018.
The reference program's roundings to bfloat16 on the way count: a program that leaves them out, or rounds other values in their place, can miss the bound.
Values may be sent and summed in bfloat16 or wider, within the bound.
A program may use at most 128 MiB of HBM per device.

```python
import math
import jax
import jax.numpy as jnp
import numpy as np
from jax import lax

NE = 200
MAP_H = 512
MAP_W = 512
BLK = 8
CAP = 2
CD = 12288
KEEP = 16
COLS = 32
NBD = 2048
SLOTS = 256
KEPT = 2048
CELLS = 196608
N_MAP = 16


def draw_kept_blocks(key, part):
    base_key = jax.random.fold_in(key, 17)

    def per_device(device_index):
        device_key = jax.random.fold_in(base_key, device_index)
        inner_set = jax.random.permutation(device_key, NBD - 2)[:KEEP - 2] + 1
        chosen = jnp.concatenate([jnp.array([0, NBD - 1], dtype=jnp.int32), inner_set.astype(jnp.int32)])
        shuffle_order = jax.random.permutation(jax.random.fold_in(device_key, 3), KEEP)
        return chosen[shuffle_order]
    return jax.vmap(per_device)(jnp.arange(N_MAP, dtype=jnp.int32)).reshape(-1).astype(jnp.int32)


def levels(key, dims, pieces, least, largest):
    factor_of, own = 1.0, jax.random.fold_in(key, 6)
    for axis_at, parts in pieces:
        draws = jnp.exp(jax.random.uniform(jax.random.fold_in(own, axis_at), (parts,), jnp.float32, least / len(pieces), largest / len(pieces)))
        factor_of = factor_of * jnp.repeat(draws, dims[axis_at] // parts).reshape([-1 if axis == axis_at else 1 for axis in range(len(dims))])
    return factor_of


def routed_block(own_key, own, number, rows, number_of, top, reach, skew):
    order = jax.random.permutation(own_key, number_of)
    crowded, ordinary = shares(number_of, rows * top, reach, skew, True), shares(number_of, rows * top, reach, skew, False)
    places = jnp.arange(number_of)

    def named(sizes, turn):
        used = int((sizes > 0).sum())
        fixed = max(1, used // 4)
        moved = fixed + (places - fixed + turn * (used - fixed)) % max(1, number_of - fixed)
        return jnp.zeros((number_of,), jnp.int32).at[order[jnp.where(places < fixed, places, moved)]].set(jnp.asarray(sizes, jnp.int32))

    sizes = jnp.where(number % 4 == 0, named(crowded, number // 4), named(ordinary, number - number // 4 - 1))
    mixed = jax.random.permutation(jax.random.fold_in(own, 3), number_of)
    giver, sink = mixed[0:number_of // 2 * 2:2], mixed[1:number_of // 2 * 2:2]
    slack = jnp.minimum(sizes[giver] - 1, reach - sizes[sink]) // 2
    slack = jnp.where((giver == order[0]) | (sink == order[0]) | (sizes[sink] == 0), 0, jnp.maximum(slack, 0))
    moved = jax.random.randint(jax.random.fold_in(own, 4), (number_of // 2,), 0, 1 << 20) % (slack + 1)
    sizes = sizes.at[giver].add(-moved).at[sink].add(moved)
    labels = jnp.searchsorted(jnp.cumsum(sizes), jnp.arange(rows * top), side="right").astype(jnp.int32)
    grid = labels.reshape(top, rows).T
    grid = grid[jax.random.permutation(jax.random.fold_in(own, 1), rows)]
    turn = jax.random.randint(jax.random.fold_in(own, 2), (rows, 1), 0, top)
    return jnp.take_along_axis(grid, (jnp.arange(top)[None, :] + turn) % top, axis=1)


def shares(count, total, most, slope, full):
    loads = [(1 << 20) // math.isqrt(rank ** slope) + 1 for rank in range(1, count + 1)]
    largest = most if full else min(most, max(-(-total // count), total * loads[0] // sum(loads)))
    least = 1 if total - largest >= count - 1 else 0
    counts, surplus = [largest] + [least] * (count - 1), total - largest - least * (count - 1)
    while surplus > 0:
        free = [i for i in range(1, count) if counts[i] < largest] or [i for i in range(1, count) if counts[i] < most]
        mass, left = sum([loads[i] for i in free]), surplus
        for i in free:
            addition = min(most - counts[i], max(1, left * loads[i] // mass), surplus)
            counts[i] = counts[i] + addition
            surplus = surplus - addition
    return np.array(counts)


def centred(key, extent, scale, reach, shards=(), kind=jnp.bfloat16):
    values = jax.random.normal(key, extent, jnp.float32) * scale
    if len(shards) > 0:
        values = levels(key, extent, shards, -0.22, 0.18) * values
    return jnp.clip(values, min=-reach, max=reach).astype(kind)


def setup_inputs(seed: int = 0, part: int = 0) -> dict:
    streams_of = jax.random.split(jax.random.key(seed), 8)
    own_keys = jax.random.split(jax.random.fold_in(streams_of[7], part), 8)
    amplitude_maps = centred(own_keys[0], (NE, MAP_H, MAP_W), 1.0, 6.0, ((1, 16),))
    kept_blocks = draw_kept_blocks(jax.random.fold_in(jax.random.fold_in(streams_of[7], part), 71), part)
    block_owner_keys = jax.random.split(jax.random.fold_in(own_keys[2], 1), (N_MAP * KEEP) // KEEP)
    block_owner_turns = jax.random.permutation(jax.random.fold_in(own_keys[2], 3), (N_MAP * KEEP) // KEEP)
    block_owner = jax.vmap(lambda own, number: routed_block(jax.random.fold_in(own_keys[2], 2), own, number, KEEP, N_MAP, 1, CAP, 2))(block_owner_keys, block_owner_turns).reshape((N_MAP * KEEP, 1))
    observed = centred(own_keys[3], (N_MAP * SLOTS,), 2.0, 8.0, ((0, 16),))
    error_scale = jnp.clip(jnp.exp(math.log(1.59375) - 1.1592369 * jax.random.uniform(own_keys[4], (N_MAP * SLOTS,), jnp.float32) ** levels(own_keys[4], (N_MAP * SLOTS,), ((0, 16),), -0.2, 0.2)), 0.5, 1.59375).astype(jnp.bfloat16)
    perturbation = centred(own_keys[5], (N_MAP * SLOTS, NE), 1.0, 6.0, ((0, 16),))
    model_slab = centred(own_keys[6], (NE, CELLS), 1.0, 6.0, ((1, 16),))
    return dict(amplitude_maps=amplitude_maps, kept_blocks=kept_blocks, block_owner=block_owner, observed=observed, error_scale=error_scale, perturbation=perturbation, model_slab=model_slab)


inflation = 4.0
epsilon = 1e-06

def dct_table(length):
    frequency = jnp.arange(length, dtype=jnp.float32)[:, None]
    sample = jnp.arange(length, dtype=jnp.float32)[None, :]
    cosine_table = jnp.cos(math.pi * (2.0 * sample + 1.0) * frequency / (2.0 * length))
    factor = jnp.where(frequency == 0, math.sqrt(1.0 / length), math.sqrt(2.0 / length))
    return (cosine_table * factor).astype(jnp.bfloat16)

def gram_terms(predicted, observed_rows, scale_rows, noise_rows, live_mask, weight_scale):
    members = predicted.shape[1]
    center = lax.optimization_barrier(jnp.mean(predicted, axis=1, keepdims=True))
    anomaly = (predicted - center) / math.sqrt(members - 1)
    weight = live_mask * weight_scale / (scale_rows * scale_rows)
    mismatch = observed_rows[:, None] + math.sqrt(inflation) * scale_rows[:, None] * noise_rows - predicted
    weighted = anomaly * weight[:, None]
    contract = (((0,), (0,)), ((), ()))
    gram_matrix = lax.dot_general(anomaly, weighted, contract, precision=lax.Precision.HIGHEST)
    cross_terms = lax.dot_general(weighted, mismatch, contract, precision=lax.Precision.HIGHEST)
    relative = mismatch / scale_rows[:, None]
    misfit_rows = live_mask * jnp.sqrt(lax.optimization_barrier(jnp.mean(relative * relative, axis=1)) + epsilon)
    return (gram_matrix, cross_terms, misfit_rows)

def solve_weights(gram_matrix, cross_terms):
    members = gram_matrix.shape[0]
    factor = jnp.linalg.cholesky(gram_matrix + inflation * jnp.eye(members, dtype=jnp.float32))
    return jax.scipy.linalg.cho_solve((factor, True), cross_terms)

def update_state(block, update_weights):
    state = block.astype(jnp.float32)
    members = state.shape[0]
    anomaly = (state - lax.optimization_barrier(jnp.mean(state, axis=0, keepdims=True))) / math.sqrt(members - 1)
    moved = state + lax.dot_general(update_weights, anomaly, (((0,), (0,)), ((), ())), precision=lax.Precision.HIGHEST)
    return moved.astype(jnp.bfloat16)

def reference(amplitude_maps, kept_blocks, block_owner, observed, error_scale, perturbation, model_slab):
    table_w = dct_table(MAP_W)
    table_h = dct_table(MAP_H)
    flat_maps = amplitude_maps.reshape(NE * MAP_H, MAP_W)
    rowwise = jnp.dot(flat_maps.astype(jnp.float32), table_w.T.astype(jnp.float32), preferred_element_type=jnp.float32).astype(jnp.bfloat16)
    rowwise = rowwise.reshape(NE, MAP_H, MAP_W).transpose(1, 0, 2).reshape(MAP_H, NE * MAP_W)
    coefficients = jnp.dot(table_h.astype(jnp.float32), rowwise.astype(jnp.float32), preferred_element_type=jnp.float32).astype(jnp.bfloat16)
    coefficients = coefficients.reshape(MAP_H, NE, MAP_W)
    per_column = MAP_H // BLK
    chosen = kept_blocks.reshape(N_MAP, KEEP)
    device_ids = jnp.arange(N_MAP, dtype=jnp.int32)[:, None]
    column_ids = device_ids * COLS + chosen // per_column
    row_starts = chosen % per_column * BLK
    within = jnp.arange(BLK, dtype=jnp.int32)
    row_ids = (row_starts[:, :, None] + within[None, None, :]).astype(jnp.int32)
    column_full = jnp.broadcast_to(column_ids[:, :, None], row_ids.shape).astype(jnp.int32)
    predicted = coefficients[row_ids, :, column_full]
    predicted = predicted.reshape(KEPT, NE).astype(jnp.float32)
    owners = block_owner.reshape(N_MAP, KEEP)
    positions = jnp.arange(KEEP, dtype=jnp.int32)
    earlier = (owners[:, :, None] == owners[:, None, :]) & (positions[None, None, :] < positions[None, :, None])
    slot_rank = lax.optimization_barrier(jnp.sum(earlier.astype(jnp.int32), axis=2))
    slot_rows = owners * SLOTS + device_ids * (CAP * BLK) + slot_rank * BLK
    data_rows = (slot_rows[:, :, None] + within[None, None, :]).reshape(KEPT).astype(jnp.int32)
    observed_rows = observed[data_rows].astype(jnp.float32)
    scale_rows = error_scale[data_rows].astype(jnp.float32)
    noise_rows = perturbation[data_rows].astype(jnp.float32)
    live_mask = jnp.ones((KEPT,), jnp.float32)
    gram_matrix, cross_terms, misfit_rows = gram_terms(predicted, observed_rows, scale_rows, noise_rows, live_mask, NE / KEPT)
    update_weights = solve_weights(gram_matrix, cross_terms)
    data_misfit = jnp.zeros((N_MAP * SLOTS,), jnp.float32).at[data_rows].set(misfit_rows)
    slab_blocks = model_slab.reshape(NE, N_MAP, CD).transpose(1, 0, 2)
    updated = lax.map(lambda block: update_state(block, update_weights), slab_blocks)
    updated_slab = updated.transpose(1, 0, 2).reshape(NE, CELLS)
    return (updated_slab, update_weights, data_misfit)
```

```python
import functools
import math

import jax
import jax.numpy as jnp
import numpy as np
from jax import lax
from jax.experimental import pallas as pl
from jax.experimental.pallas import tpu as pltpu
from jax.sharding import PartitionSpec as P

BLK = 8
CAP = 2
LANES = 128


inflation = 4.0
epsilon = 1e-06
MESH = pl.DeviceIdType.MESH
VMEM = pltpu.VMEM


def dct_table(length):
    frequency = jnp.arange(length, dtype=jnp.float32)[:, None]
    sample = jnp.arange(length, dtype=jnp.float32)[None, :]
    cosine_table = jnp.cos(math.pi * (2.0 * sample + 1.0) * frequency / (2.0 * length))
    factor = jnp.where(frequency == 0, math.sqrt(1.0 / length), math.sqrt(2.0 / length))
    return (cosine_table * factor).astype(jnp.bfloat16)


def dct_constant(length):
    f32 = np.float32
    frequency = np.arange(length, dtype=f32)[:, None]
    sample = np.arange(length, dtype=f32)[None, :]
    angle = f32(math.pi) * (f32(2) * sample + f32(1)) * frequency / f32(2 * length)
    cosine_table = np.cos(angle.astype(np.float64)).astype(f32)
    factor = np.where(frequency == 0, f32(math.sqrt(1.0 / length)), f32(math.sqrt(2.0 / length)))
    return (cosine_table * factor).astype(jnp.bfloat16)


def gram_terms(predicted, observed_rows, scale_rows, noise_rows, live_mask, weight_scale):
    members = predicted.shape[1]
    center = jnp.mean(predicted, axis=1, keepdims=True)
    anomaly = (predicted - center) / math.sqrt(members - 1)
    weight = live_mask * weight_scale / (scale_rows * scale_rows)
    mismatch = (
        observed_rows[:, None] + math.sqrt(inflation) * scale_rows[:, None] * noise_rows - predicted
    )
    weighted = anomaly * weight[:, None]
    contract = (((0,), (0,)), ((), ()))
    gram_matrix = lax.dot_general(anomaly, weighted, contract, precision=lax.Precision.HIGHEST)
    cross_terms = lax.dot_general(weighted, mismatch, contract, precision=lax.Precision.HIGHEST)
    relative = mismatch / scale_rows[:, None]
    misfit_rows = live_mask * jnp.sqrt(jnp.mean(relative * relative, axis=1) + epsilon)
    return (gram_matrix, cross_terms, misfit_rows)


def solve_weights(gram_matrix, cross_terms):
    members = gram_matrix.shape[0]
    factor = jnp.linalg.cholesky(gram_matrix + inflation * jnp.eye(members, dtype=jnp.float32))
    return jax.scipy.linalg.cho_solve((factor, True), cross_terms)


def update_state(block, update_weights):
    state = block.astype(jnp.float32)
    members = state.shape[0]
    anomaly = (state - jnp.mean(state, axis=0, keepdims=True)) / math.sqrt(members - 1)
    moved = state + lax.dot_general(
        update_weights, anomaly, (((0,), (0,)), ((), ())), precision=lax.Precision.HIGHEST
    )
    return moved.astype(jnp.bfloat16)


def body_large(amplitude_maps, kept_blocks, block_owner, observed, error_scale, perturbation, model_slab):
    members, rows_here, map_width = amplitude_maps.shape
    devices = lax.axis_size("map")
    map_height = rows_here * devices
    table_w = dct_table(map_width)
    table_h = dct_table(map_height)
    rowwise = jnp.einsum(
        "ehw,kw->hke", amplitude_maps, table_w, preferred_element_type=jnp.float32
    ).astype(jnp.bfloat16)
    coefficients = jnp.einsum(
        "kh,hwe->wke",
        table_h,
        lax.all_to_all(rowwise, "map", split_axis=1, concat_axis=0, tiled=True),
        preferred_element_type=jnp.float32,
    ).astype(jnp.bfloat16)
    block_rows = coefficients.reshape(-1, BLK * members)
    candidates = block_rows.shape[0]
    keep_count = kept_blocks.shape[0]
    slot_count = devices * CAP
    dest_owner = block_owner[:, 0]
    positions = jnp.arange(keep_count, dtype=jnp.int32)
    earlier = (dest_owner[:, None] == dest_owner[None, :]) & (
        positions[None, :] < positions[:, None]
    )
    slot_rank = jnp.sum(earlier.astype(jnp.int32), axis=1)
    slot_index = dest_owner * CAP + slot_rank
    pick_slot = (slot_index[:, None] == jnp.arange(slot_count, dtype=jnp.int32)[None, :]).astype(
        jnp.bfloat16
    )
    weight_scale = members / (devices * keep_count * BLK)
    contract = (((0,), (0,)), ((), ()))
    pick_block = (kept_blocks[:, None] == jnp.arange(candidates, dtype=jnp.int32)[None, :]).astype(
        jnp.bfloat16
    )
    routing = lax.dot_general(
        pick_slot, pick_block, contract, preferred_element_type=jnp.float32
    ).astype(jnp.bfloat16)
    outgoing = jnp.dot(routing, block_rows, preferred_element_type=jnp.float32).astype(jnp.bfloat16)
    live_slots = jnp.sum(pick_slot.astype(jnp.float32), axis=0).astype(jnp.bfloat16)
    arrived, arrived_live = (
        lax.all_to_all(
            outgoing.reshape(devices, CAP, BLK * members),
            "map",
            split_axis=0,
            concat_axis=0,
            tiled=True,
        ),
        lax.all_to_all(
            live_slots.reshape(devices, CAP), "map", split_axis=0, concat_axis=0, tiled=True
        ),
    )
    predicted = arrived.reshape(-1, members).astype(jnp.float32)
    live_mask = jnp.repeat(arrived_live.astype(jnp.float32).reshape(-1), BLK)
    gram_matrix, cross_terms, data_misfit = gram_terms(
        predicted,
        observed.astype(jnp.float32),
        error_scale.astype(jnp.float32),
        perturbation.astype(jnp.float32),
        live_mask,
        weight_scale,
    )
    gram_matrix, cross_terms = lax.psum((gram_matrix, cross_terms), "map")
    update_weights = solve_weights(gram_matrix, cross_terms)
    updated_slab = update_state(model_slab, update_weights)
    return (updated_slab, update_weights, data_misfit)


def transform_kernel(rows_here, maps_ref, row_table_ref, column_table_ref, part_ref, rowwise_ref):
    chunk, _, width = maps_ref.shape
    flat = maps_ref[...].reshape(chunk * rows_here, width)
    rowwise = lax.dot_general(
        flat, row_table_ref[...], (((1,), (1,)), ((), ())), preferred_element_type=jnp.float32
    )
    halves = rowwise_ref.shape[0]
    for half in range(halves):
        rowwise_ref[half] = rowwise[:, half * LANES : (half + 1) * LANES]

    def tile(t, carry):
        for half in range(halves):
            lanes = slice(half * LANES, (half + 1) * LANES)
            total = [None] * BLK
            for h in range(rows_here):
                row = rowwise_ref[half, pl.ds(t * 8 * rows_here + h, 8, stride=rows_here), :]
                row = row.astype(jnp.bfloat16).astype(jnp.float32)
                for c in range(BLK):
                    term = row * column_table_ref[h, c : c + 1, lanes]
                    total[c] = term if total[c] is None else total[c] + term
            for c in range(BLK):
                part_ref[c * halves + half, pl.ds(pl.multiple_of(t * 8, 8), 8), :] = total[c]
        return carry

    lax.fori_loop(0, chunk // 8, tile, 0)


def transform(maps, row_table, column_table):
    members, rows_here, width = maps.shape
    blocks = row_table.shape[0]
    chunk = 40
    pieces = BLK * blocks // LANES
    return pl.pallas_call(
        functools.partial(transform_kernel, rows_here),
        grid=(members // chunk,),
        out_shape=jax.ShapeDtypeStruct((pieces, members, LANES), jnp.float32),
        in_specs=[
            pl.BlockSpec((chunk, rows_here, width), lambda i: (i, 0, 0)),
            pl.BlockSpec((blocks, width), lambda i: (0, 0)),
            pl.BlockSpec((rows_here, BLK, blocks), lambda i: (0, 0, 0)),
        ],
        out_specs=pl.BlockSpec((pieces, chunk, LANES), lambda i: (0, i, 0)),
        scratch_shapes=[VMEM((blocks // LANES, chunk * rows_here, LANES), jnp.float32)],
        compiler_params=pltpu.CompilerParams(vmem_limit_bytes=40 * 2**20),
        name="transform",
    )(maps, row_table, column_table)


def combine_kernel(
    part_ref, out_ref, held, from_core, from_x, from_z, sends, recvs
):
    members = part_ref.shape[1]
    me = lax.axis_index("map")
    core = lax.rem(me, 2)
    x = lax.rem(me // 2, 2)
    z = me // 4
    core_peer = me + 1 - 2 * core
    x_peer = me + 2 - 4 * x
    z_peers = [lax.rem(z + s, 4) * 4 + x * 2 + core for s in (1, 2, 3)]

    barrier = pltpu.get_barrier_semaphore()
    for peer in [core_peer, x_peer] + z_peers:
        pl.semaphore_signal(barrier, inc=1, device_id={"map": peer}, device_id_type=MESH)
    pl.semaphore_wait(barrier, 5)

    def send(number, src, dst, peer):
        copy = pltpu.make_async_remote_copy(
            src_ref=src,
            dst_ref=dst,
            send_sem=sends.at[number],
            recv_sem=recvs.at[number],
            device_id={"map": peer},
            device_id_type=MESH,
        )
        copy.start()
        return copy

    first = []
    for xi in range(2):
        xx = 1 - x if xi == 0 else x
        for zi in range(4):
            n = xi * 4 + zi
            first.append(
                send(n, part_ref.at[zi * 4 + xx * 2 + 1 - core], from_core.at[n], core_peer)
            )
    second = []
    for n in range(4):
        first[n].wait_recv()
        held[n] = part_ref[n * 4 + (1 - x) * 2 + core] + from_core[n]
        second.append(send(8 + n, held.at[n], from_x.at[n], x_peer))
    third = []
    for s in (1, 2, 3, 0):
        zi = lax.rem(z + s, 4)
        if s == 1:
            for n in range(4):
                first[4 + n].wait_recv()
                second[n].wait_recv()
        held[4 + s] = part_ref[zi * 4 + x * 2 + core] + from_core[4 + zi] + from_x[zi]
        if s:
            third.append(send(12 + s - 1, held.at[4 + s], from_z.at[s - 1], z_peers[s - 1]))
    for copy in third:
        copy.wait_recv()
    total = held[4] + from_z[0] + from_z[1] + from_z[2]
    pad = out_ref.shape[1] - members
    mine = jnp.concatenate([total, jnp.zeros((pad, LANES), jnp.float32)], axis=0)
    out_ref[me] = mine.astype(jnp.bfloat16)

    fourth = [send(15 + s, out_ref.at[me], out_ref.at[me], z_peers[s]) for s in range(3)]
    fifth = [send(18, out_ref.at[me], out_ref.at[me], x_peer)]
    sixth = [send(22, out_ref.at[me], out_ref.at[me], core_peer)]
    for s in range(3):
        fourth[s].wait_recv()
        piece = lax.rem(z + 3 - s, 4) * 4 + x * 2 + core
        fifth.append(send(19 + s, out_ref.at[piece], out_ref.at[piece], x_peer))
        sixth.append(send(23 + s, out_ref.at[piece], out_ref.at[piece], core_peer))
    for n in range(4):
        fifth[n].wait_recv()
        piece = lax.rem(z + 4 - n, 4) * 4 + (1 - x) * 2 + core
        sixth.append(send(26 + n, out_ref.at[piece], out_ref.at[piece], core_peer))
    for copy in sixth:
        copy.wait_recv()
    for copy in first + second + third + fourth + fifth + sixth:
        copy.wait_send()


def combine(parts):
    pieces, members, _ = parts.shape
    padded = -(-members // 16) * 16
    piece = (members, LANES)
    return pl.pallas_call(
        combine_kernel,
        out_shape=jax.ShapeDtypeStruct((pieces, padded, LANES), jnp.bfloat16),
        in_specs=[pl.BlockSpec(memory_space=VMEM)],
        out_specs=pl.BlockSpec(memory_space=VMEM),
        scratch_shapes=[
            VMEM((8,) + piece, jnp.float32),
            VMEM((8,) + piece, jnp.float32),
            VMEM((4,) + piece, jnp.float32),
            VMEM((3,) + piece, jnp.float32),
            pltpu.SemaphoreType.DMA((30,)),
            pltpu.SemaphoreType.DMA((30,)),
        ],
        compiler_params=pltpu.CompilerParams(
            collective_id=0, has_side_effects=True, vmem_limit_bytes=40 * 2**20
        ),
        name="combine",
    )(parts)


def solve_kernel(
    weight_scale, predicted_ref, data_ref, weights_ref, high_ref, low_ref, misfit_ref,
    weighted, paired, system,
):
    pieces = predicted_ref.shape[0]
    members = weights_ref.shape[0]
    halves = data_ref.shape[2] // LANES
    wide = 256
    for n in range(pieces):
        c, half = divmod(n, halves)
        lanes = slice(half * LANES, (half + 1) * LANES)
        here = slice(n * LANES, (n + 1) * LANES)
        predicted = predicted_ref[n].astype(jnp.float32)[:members]
        data = data_ref[c, :, lanes].astype(jnp.float32)
        noise = data[:members]
        observed = data[members : members + 1]
        scale = data[members + 1 : members + 2]
        center = jnp.sum(predicted, axis=0, keepdims=True) / members
        anomaly = (predicted - center) / math.sqrt(members - 1)
        weight = weight_scale / (scale * scale)
        mismatch = observed + math.sqrt(inflation) * scale * noise - predicted
        relative = mismatch / scale
        misfit_ref[c : c + 1, lanes] = jnp.sqrt(
            jnp.sum(relative * relative, axis=0, keepdims=True) / members + epsilon
        )
        weighted[:, here] = anomaly * weight
        paired[0:members, here] = anomaly
        paired[wide : wide + members, here] = mismatch
    contract = (((1,), (1,)), ((), ()))
    for part in range(2):
        rows = slice(part * wide, part * wide + members)
        product = lax.dot_general(
            weighted[...], paired[rows, :], contract,
            preferred_element_type=jnp.float32, precision=lax.Precision.HIGHEST,
        )
        if part == 0:
            i = lax.broadcasted_iota(jnp.int32, product.shape, 0)
            j = lax.broadcasted_iota(jnp.int32, product.shape, 1)
            product = product + jnp.where(i == j, inflation, 0.0)
        system[:, part * wide : part * wide + members] = product
    width = system.shape[1]
    sub = lax.broadcasted_iota(jnp.int32, (8, 1), 0)
    row_number = lax.broadcasted_iota(jnp.int32, (members, 1), 0)
    for k in range(members // 8):
        start = 8 * k
        low = start // LANES * LANES
        block = system[start : start + 8, low:width]
        for j in range(8):
            at = start - low + j
            column = block[:, at : at + 1]
            pivot = block[j : j + 1, :] / column[j : j + 1, :]
            block = jnp.where(sub == j, pivot, block - column * pivot)
        columns = system[:, start : start + 8]
        outside = (row_number < start) | (row_number >= start + 8)
        columns = jnp.where(outside, columns, 0.0)
        system[:, low:width] = system[:, low:width] - jnp.dot(
            columns, block, preferred_element_type=jnp.float32, precision=lax.Precision.HIGHEST
        )
        system[start : start + 8, low:width] = block
    solved = system[:, wide : wide + members]
    weights_ref[...] = solved
    centred = (solved - jnp.sum(solved, axis=0, keepdims=True) / members) / math.sqrt(members - 1)
    turned = centred.T
    high = turned.astype(jnp.bfloat16)
    high_ref[...] = high
    low_ref[...] = (turned - high.astype(jnp.float32)).astype(jnp.bfloat16)


def solve(predicted, data, members, weight_scale):
    pieces = predicted.shape[0]
    cells = pieces * LANES
    square = (members, members)
    return pl.pallas_call(
        functools.partial(solve_kernel, weight_scale),
        out_shape=(
            jax.ShapeDtypeStruct(square, jnp.float32),
            jax.ShapeDtypeStruct(square, jnp.bfloat16),
            jax.ShapeDtypeStruct(square, jnp.bfloat16),
            jax.ShapeDtypeStruct((data.shape[0], data.shape[2]), jnp.float32),
        ),
        in_specs=[pl.BlockSpec(memory_space=VMEM)] * 2,
        out_specs=(pl.BlockSpec(memory_space=VMEM),) * 4,
        scratch_shapes=[
            VMEM((members, cells), jnp.float32),
            VMEM((256 + members, cells), jnp.float32),
            VMEM((members, 512), jnp.float32),
        ],
        compiler_params=pltpu.CompilerParams(vmem_limit_bytes=40 * 2**20),
        name="solve",
    )(predicted, data)


def update_kernel(high_ref, low_ref, slab_ref, out_ref):
    state = slab_ref[...]
    moved = jnp.dot(high_ref[...], state, preferred_element_type=jnp.float32)
    moved = moved + jnp.dot(low_ref[...], state, preferred_element_type=jnp.float32)
    out_ref[...] = (state.astype(jnp.float32) + moved).astype(jnp.bfloat16)


def update(high, low, slab):
    members, cells = slab.shape
    tile = 1024
    whole = pl.BlockSpec((members, members), lambda i: (0, 0))
    column = pl.BlockSpec((members, tile), lambda i: (0, i))
    return pl.pallas_call(
        update_kernel,
        grid=(cells // tile,),
        out_shape=jax.ShapeDtypeStruct(slab.shape, jnp.bfloat16),
        in_specs=[whole, whole, column],
        out_specs=column,
        compiler_params=pltpu.CompilerParams(vmem_limit_bytes=40 * 2**20),
        name="update",
    )(high, low, slab)


def body_small(amplitude_maps, kept_blocks, block_owner, observed, error_scale, perturbation, model_slab):
    members, rows_here, map_width = amplitude_maps.shape
    devices = lax.axis_size("map")
    me = lax.axis_index("map")
    map_height = rows_here * devices
    keep_count = kept_blocks.shape[0]
    columns_here = map_width // devices
    per_column = map_height // BLK
    table_w = jnp.asarray(dct_constant(map_width))
    table_h = jnp.asarray(dct_constant(map_height))

    names = jnp.stack([kept_blocks, block_owner[:, 0]])
    names = lax.all_gather(names, "map")
    local = jnp.concatenate(
        [perturbation, observed[:, None], error_scale[:, None]], axis=1
    )
    local = lax.all_gather(local, "map", tiled=True)

    blocks = names[:, 0, :].reshape(-1)
    owners = names[:, 1, :]
    source = jnp.repeat(jnp.arange(devices, dtype=jnp.int32), keep_count)
    column_of = source * columns_here + blocks // per_column
    row_of = blocks % per_column
    one = jnp.bfloat16
    pick_column = (column_of[:, None] == jnp.arange(map_width, dtype=jnp.int32)[None, :]).astype(one)
    row_table = jnp.dot(pick_column, table_w, preferred_element_type=jnp.float32).astype(one)
    pick_row = (row_of[:, None] == jnp.arange(per_column, dtype=jnp.int32)[None, :]).astype(one)
    here = lax.dynamic_slice_in_dim(table_h, me * rows_here, rows_here, axis=1)
    column_table = jnp.einsum(
        "bk,kch->hcb",
        pick_row,
        here.reshape(per_column, BLK, rows_here),
        preferred_element_type=jnp.float32,
    )
    parts = transform(amplitude_maps, row_table, column_table)
    predicted = combine(parts)

    positions = jnp.arange(keep_count, dtype=jnp.int32)
    earlier = (owners[:, :, None] == owners[:, None, :]) & (
        positions[None, None, :] < positions[None, :, None]
    )
    rank = jnp.sum(earlier.astype(jnp.int32), axis=2)
    slot = ((owners * devices + jnp.arange(devices, dtype=jnp.int32)[:, None]) * CAP + rank).reshape(-1)
    slots = devices * devices * CAP
    pick_slot = (jnp.arange(slots, dtype=jnp.int32)[:, None] == slot[None, :]).astype(one)
    data = jnp.einsum(
        "sce,sb->ceb",
        local.reshape(slots, BLK, members + 2),
        pick_slot,
        preferred_element_type=jnp.float32,
    ).astype(one)
    weight_scale = members / (devices * keep_count * BLK)
    update_weights, high, low, misfit = solve(predicted, data, members, weight_scale)
    updated_slab = update(high, low, model_slab)
    mine = lax.dynamic_slice_in_dim(pick_slot, me * devices * CAP, devices * CAP, axis=0)
    data_misfit = jnp.einsum(
        "sb,cb->sc", mine.astype(jnp.float32), misfit, precision=lax.Precision.HIGHEST
    ).reshape(-1)
    return (updated_slab, update_weights, data_misfit)


def solution(mesh):
    in_specs = (
        P("groups", "map", None),
        P(("groups", "map")),
        P(("groups", "map"), None),
        P(("groups", "map")),
        P(("groups", "map")),
        P(("groups", "map"), None),
        P(None, ("groups", "map")),
    )
    out_specs = (P(None, ("groups", "map")), P("groups", None), P(("groups", "map")))
    devices = mesh.shape["map"]

    def run(*args):
        kept = args[1].shape[0] // mesh.shape["groups"]
        fits = devices == 16 and kept * BLK == devices * LANES
        body = body_small if fits else body_large
        return jax.shard_map(body, mesh=mesh, in_specs=in_specs, out_specs=out_specs, check_vma=False)(*args)

    return run
```

```python
import functools
import math

import jax
import jax.numpy as jnp
import numpy as np
from jax import lax
from jax.experimental import pallas as pl
from jax.experimental.pallas import tpu as pltpu
from jax.sharding import PartitionSpec as P

BLK = 8
CAP = 2
LANES = 128


inflation = 4.0
epsilon = 1e-06
MESH = pl.DeviceIdType.MESH
VMEM = pltpu.VMEM


def dct_table(length):
    frequency = jnp.arange(length, dtype=jnp.float32)[:, None]
    sample = jnp.arange(length, dtype=jnp.float32)[None, :]
    cosine_table = jnp.cos(math.pi * (2.0 * sample + 1.0) * frequency / (2.0 * length))
    factor = jnp.where(frequency == 0, math.sqrt(1.0 / length), math.sqrt(2.0 / length))
    return (cosine_table * factor).astype(jnp.bfloat16)


def dct_constant(length):
    f32 = np.float32
    frequency = np.arange(length, dtype=f32)[:, None]
    sample = np.arange(length, dtype=f32)[None, :]
    angle = f32(math.pi) * (f32(2) * sample + f32(1)) * frequency / f32(2 * length)
    cosine_table = np.cos(angle.astype(np.float64)).astype(f32)
    factor = np.where(frequency == 0, f32(math.sqrt(1.0 / length)), f32(math.sqrt(2.0 / length)))
    return (cosine_table * factor).astype(jnp.bfloat16)


def gram_terms(predicted, observed_rows, scale_rows, noise_rows, live_mask, weight_scale):
    members = predicted.shape[1]
    center = jnp.mean(predicted, axis=1, keepdims=True)
    anomaly = (predicted - center) / math.sqrt(members - 1)
    weight = live_mask * weight_scale / (scale_rows * scale_rows)
    mismatch = (
        observed_rows[:, None] + math.sqrt(inflation) * scale_rows[:, None] * noise_rows - predicted
    )
    weighted = anomaly * weight[:, None]
    contract = (((0,), (0,)), ((), ()))
    gram_matrix = lax.dot_general(anomaly, weighted, contract, precision=lax.Precision.HIGHEST)
    cross_terms = lax.dot_general(weighted, mismatch, contract, precision=lax.Precision.HIGHEST)
    relative = mismatch / scale_rows[:, None]
    misfit_rows = live_mask * jnp.sqrt(jnp.mean(relative * relative, axis=1) + epsilon)
    return (gram_matrix, cross_terms, misfit_rows)


def solve_weights(gram_matrix, cross_terms):
    members = gram_matrix.shape[0]
    factor = jnp.linalg.cholesky(gram_matrix + inflation * jnp.eye(members, dtype=jnp.float32))
    return jax.scipy.linalg.cho_solve((factor, True), cross_terms)


def update_state(block, update_weights):
    state = block.astype(jnp.float32)
    members = state.shape[0]
    anomaly = (state - jnp.mean(state, axis=0, keepdims=True)) / math.sqrt(members - 1)
    moved = state + lax.dot_general(
        update_weights, anomaly, (((0,), (0,)), ((), ())), precision=lax.Precision.HIGHEST
    )
    return moved.astype(jnp.bfloat16)


def body_large(amplitude_maps, kept_blocks, block_owner, observed, error_scale, perturbation, model_slab):
    members, rows_here, map_width = amplitude_maps.shape
    devices = lax.axis_size("map")
    map_height = rows_here * devices
    table_w = dct_table(map_width)
    table_h = dct_table(map_height)
    rowwise = jnp.einsum(
        "ehw,kw->hke", amplitude_maps, table_w, preferred_element_type=jnp.float32
    ).astype(jnp.bfloat16)
    coefficients = jnp.einsum(
        "kh,hwe->wke",
        table_h,
        lax.all_to_all(rowwise, "map", split_axis=1, concat_axis=0, tiled=True),
        preferred_element_type=jnp.float32,
    ).astype(jnp.bfloat16)
    block_rows = coefficients.reshape(-1, BLK * members)
    candidates = block_rows.shape[0]
    keep_count = kept_blocks.shape[0]
    slot_count = devices * CAP
    dest_owner = block_owner[:, 0]
    positions = jnp.arange(keep_count, dtype=jnp.int32)
    earlier = (dest_owner[:, None] == dest_owner[None, :]) & (
        positions[None, :] < positions[:, None]
    )
    slot_rank = jnp.sum(earlier.astype(jnp.int32), axis=1)
    slot_index = dest_owner * CAP + slot_rank
    pick_slot = (slot_index[:, None] == jnp.arange(slot_count, dtype=jnp.int32)[None, :]).astype(
        jnp.bfloat16
    )
    weight_scale = members / (devices * keep_count * BLK)
    contract = (((0,), (0,)), ((), ()))
    pick_block = (kept_blocks[:, None] == jnp.arange(candidates, dtype=jnp.int32)[None, :]).astype(
        jnp.bfloat16
    )
    routing = lax.dot_general(
        pick_slot, pick_block, contract, preferred_element_type=jnp.float32
    ).astype(jnp.bfloat16)
    outgoing = jnp.dot(routing, block_rows, preferred_element_type=jnp.float32).astype(jnp.bfloat16)
    live_slots = jnp.sum(pick_slot.astype(jnp.float32), axis=0).astype(jnp.bfloat16)
    arrived, arrived_live = (
        lax.all_to_all(
            outgoing.reshape(devices, CAP, BLK * members),
            "map",
            split_axis=0,
            concat_axis=0,
            tiled=True,
        ),
        lax.all_to_all(
            live_slots.reshape(devices, CAP), "map", split_axis=0, concat_axis=0, tiled=True
        ),
    )
    predicted = arrived.reshape(-1, members).astype(jnp.float32)
    live_mask = jnp.repeat(arrived_live.astype(jnp.float32).reshape(-1), BLK)
    gram_matrix, cross_terms, data_misfit = gram_terms(
        predicted,
        observed.astype(jnp.float32),
        error_scale.astype(jnp.float32),
        perturbation.astype(jnp.float32),
        live_mask,
        weight_scale,
    )
    gram_matrix, cross_terms = lax.psum((gram_matrix, cross_terms), "map")
    update_weights = solve_weights(gram_matrix, cross_terms)
    updated_slab = update_state(model_slab, update_weights)
    return (updated_slab, update_weights, data_misfit)


def transform_kernel(rows_here, maps_ref, row_table_ref, column_table_ref, part_ref, rowwise_ref):
    chunk, _, width = maps_ref.shape
    flat = maps_ref[...].reshape(chunk * rows_here, width)
    rowwise = lax.dot_general(
        flat, row_table_ref[...], (((1,), (1,)), ((), ())), preferred_element_type=jnp.float32
    )
    halves = rowwise_ref.shape[0]
    for half in range(halves):
        rowwise_ref[half] = rowwise[:, half * LANES : (half + 1) * LANES]

    def tile(t, carry):
        for half in range(halves):
            lanes = slice(half * LANES, (half + 1) * LANES)
            total = [None] * BLK
            for h in range(rows_here):
                row = rowwise_ref[half, pl.ds(t * 8 * rows_here + h, 8, stride=rows_here), :]
                row = row.astype(jnp.bfloat16).astype(jnp.float32)
                for c in range(BLK):
                    term = row * column_table_ref[h, c : c + 1, lanes]
                    total[c] = term if total[c] is None else total[c] + term
            for c in range(BLK):
                part_ref[c * halves + half, pl.ds(pl.multiple_of(t * 8, 8), 8), :] = total[c]
        return carry

    lax.fori_loop(0, chunk // 8, tile, 0)


def transform(maps, row_table, column_table):
    members, rows_here, width = maps.shape
    blocks = row_table.shape[0]
    chunk = 40
    pieces = BLK * blocks // LANES
    return pl.pallas_call(
        functools.partial(transform_kernel, rows_here),
        grid=(members // chunk,),
        out_shape=jax.ShapeDtypeStruct((pieces, members, LANES), jnp.float32),
        in_specs=[
            pl.BlockSpec((chunk, rows_here, width), lambda i: (i, 0, 0)),
            pl.BlockSpec((blocks, width), lambda i: (0, 0)),
            pl.BlockSpec((rows_here, BLK, blocks), lambda i: (0, 0, 0)),
        ],
        out_specs=pl.BlockSpec((pieces, chunk, LANES), lambda i: (0, i, 0)),
        scratch_shapes=[VMEM((blocks // LANES, chunk * rows_here, LANES), jnp.float32)],
        compiler_params=pltpu.CompilerParams(vmem_limit_bytes=58 * 2**20),
        name="transform",
    )(maps, row_table, column_table)


def names_kernel(names_ref, all_ref, sends, recvs):
    devices = all_ref.shape[0]
    me = lax.axis_index("map")
    peers = [lax.rem(me + s, devices) for s in range(1, devices)]
    barrier = pltpu.get_barrier_semaphore()
    for peer in peers:
        pl.semaphore_signal(barrier, inc=1, device_id={"map": peer}, device_id_type=MESH)
    pl.semaphore_wait(barrier, devices - 1)
    copies = []
    for s, peer in enumerate(peers):
        copy = pltpu.make_async_remote_copy(
            src_ref=names_ref,
            dst_ref=all_ref.at[me],
            send_sem=sends.at[s],
            recv_sem=recvs.at[s],
            device_id={"map": peer},
            device_id_type=MESH,
        )
        copy.start()
        copies.append(copy)
    all_ref[me] = names_ref[...]
    for copy in copies:
        copy.wait()


def gather_names(names, devices):
    return pl.pallas_call(
        names_kernel,
        out_shape=jax.ShapeDtypeStruct((devices,) + names.shape, names.dtype),
        in_specs=[pl.BlockSpec(memory_space=VMEM)],
        out_specs=pl.BlockSpec(memory_space=VMEM),
        scratch_shapes=[
            pltpu.SemaphoreType.DMA((devices - 1,)),
            pltpu.SemaphoreType.DMA((devices - 1,)),
        ],
        compiler_params=pltpu.CompilerParams(collective_id=1, has_side_effects=True),
        name="names",
    )(names)


def combine_kernel(
    part_ref, out_ref, held, from_core, from_x, from_z, sends, recvs
):
    members = part_ref.shape[1]
    me = lax.axis_index("map")
    core = lax.rem(me, 2)
    x = lax.rem(me // 2, 2)
    z = me // 4
    core_peer = me + 1 - 2 * core
    x_peer = me + 2 - 4 * x
    z_peers = [lax.rem(z + s, 4) * 4 + x * 2 + core for s in (1, 2, 3)]

    barrier = pltpu.get_barrier_semaphore()
    for peer in [core_peer, x_peer] + z_peers:
        pl.semaphore_signal(barrier, inc=1, device_id={"map": peer}, device_id_type=MESH)
    pl.semaphore_wait(barrier, 5)

    def send(number, src, dst, peer):
        copy = pltpu.make_async_remote_copy(
            src_ref=src,
            dst_ref=dst,
            send_sem=sends.at[number],
            recv_sem=recvs.at[number],
            device_id={"map": peer},
            device_id_type=MESH,
        )
        copy.start()
        return copy

    order = (2, 1, 3, 0)
    zs = [lax.rem(z + s, 4) for s in order]
    first = []
    for n in range(8):
        xx = 1 - x if n < 4 else x
        piece = zs[n % 4] * 4 + xx * 2 + 1 - core
        first.append(send(n, part_ref.at[piece], from_core.at[n], core_peer))
    second = []
    for n in range(4):
        first[n].wait_recv()
        held[n] = part_ref[zs[n] * 4 + (1 - x) * 2 + core] + from_core[n]
        second.append(send(8 + n, held.at[n], from_x.at[n], x_peer))
    third = []
    for n, s in enumerate(order):
        first[4 + n].wait_recv()
        own = part_ref[zs[n] * 4 + x * 2 + core] + from_core[4 + n]
        second[n].wait_recv()
        held[4 + n] = own + from_x[n]
        if s:
            third.append(send(12 + n, held.at[4 + n], from_z.at[n], z_peers[s - 1]))
    for copy in third:
        copy.wait_recv()
    total = held[7] + from_z[0] + from_z[1] + from_z[2]
    pad = out_ref.shape[1] - members
    mine = jnp.concatenate([total, jnp.zeros((pad, LANES), jnp.float32)], axis=0)
    out_ref[me] = mine.astype(jnp.bfloat16)

    fourth = [send(15 + s, out_ref.at[me], out_ref.at[me], z_peers[s]) for s in range(3)]
    fifth = [send(18, out_ref.at[me], out_ref.at[me], x_peer)]
    sixth = [send(22, out_ref.at[me], out_ref.at[me], core_peer)]
    for s in range(3):
        fourth[s].wait_recv()
        piece = lax.rem(z + 3 - s, 4) * 4 + x * 2 + core
        fifth.append(send(19 + s, out_ref.at[piece], out_ref.at[piece], x_peer))
        sixth.append(send(23 + s, out_ref.at[piece], out_ref.at[piece], core_peer))
    for n in range(4):
        fifth[n].wait_recv()
        piece = lax.rem(z + 4 - n, 4) * 4 + (1 - x) * 2 + core
        sixth.append(send(26 + n, out_ref.at[piece], out_ref.at[piece], core_peer))
    for copy in sixth:
        copy.wait_recv()
    for copy in first + second + third + fourth + fifth + sixth:
        copy.wait_send()


def combine(parts):
    pieces, members, _ = parts.shape
    padded = -(-members // 16) * 16
    piece = (members, LANES)
    return pl.pallas_call(
        combine_kernel,
        out_shape=jax.ShapeDtypeStruct((pieces, padded, LANES), jnp.bfloat16),
        in_specs=[pl.BlockSpec(memory_space=VMEM)],
        out_specs=pl.BlockSpec(memory_space=VMEM),
        scratch_shapes=[
            VMEM((8,) + piece, jnp.float32),
            VMEM((8,) + piece, jnp.float32),
            VMEM((4,) + piece, jnp.float32),
            VMEM((3,) + piece, jnp.float32),
            pltpu.SemaphoreType.DMA((30,)),
            pltpu.SemaphoreType.DMA((30,)),
        ],
        compiler_params=pltpu.CompilerParams(
            collective_id=0, has_side_effects=True, vmem_limit_bytes=40 * 2**20
        ),
        name="combine",
    )(parts)


def solve_kernel(
    weight_scale, predicted_ref, data_ref, slab_ref, updated_ref, weights_ref, misfit_ref,
    weighted, paired, system, slab, reads, writes,
):
    pieces = predicted_ref.shape[0]
    members = weights_ref.shape[0]
    halves = data_ref.shape[2] // LANES
    wide = 256
    tiles = reads.shape[0]
    tile = slab.shape[1] // tiles
    fetches = []
    for n in range(tiles):
        here = slice(n * tile, (n + 1) * tile)
        fetch = pltpu.make_async_copy(slab_ref.at[:, here], slab.at[:, here], reads.at[n])
        fetch.start()
        fetches.append(fetch)
    for n in range(pieces):
        c, half = divmod(n, halves)
        lanes = slice(half * LANES, (half + 1) * LANES)
        here = slice(n * LANES, (n + 1) * LANES)
        predicted = predicted_ref[n].astype(jnp.float32)[:members]
        data = data_ref[c, :, lanes].astype(jnp.float32)
        noise = data[:members]
        observed = data[members : members + 1]
        scale = data[members + 1 : members + 2]
        center = jnp.sum(predicted, axis=0, keepdims=True) / members
        anomaly = (predicted - center) * (1.0 / math.sqrt(members - 1))
        weight = weight_scale / (scale * scale)
        mismatch = observed + math.sqrt(inflation) * scale * noise - predicted
        squares = jnp.sum(mismatch * mismatch, axis=0, keepdims=True) / (scale * scale)
        misfit_ref[c : c + 1, lanes] = jnp.sqrt(squares / members + epsilon)
        weighted[:, here] = anomaly * weight
        paired[0:members, here] = anomaly
        paired[wide : wide + members, here] = mismatch
    contract = (((1,), (1,)), ((), ()))
    for part in range(2):
        rows = slice(part * wide, part * wide + members)
        product = lax.dot_general(
            weighted[...], paired[rows, :], contract,
            preferred_element_type=jnp.float32, precision=lax.Precision.HIGHEST,
        )
        if part == 0:
            i = lax.broadcasted_iota(jnp.int32, product.shape, 0)
            j = lax.broadcasted_iota(jnp.int32, product.shape, 1)
            product = product + jnp.where(i == j, inflation, 0.0)
        system[:, part * wide : part * wide + members] = product
    width = system.shape[1]
    sub = lax.broadcasted_iota(jnp.int32, (8, 1), 0)
    row_number = lax.broadcasted_iota(jnp.int32, (members, 1), 0)
    block = system[0:8, :]
    for k in range(members // 8):
        start = 8 * k
        low = start // LANES * LANES
        for j in range(8):
            at = start - low + j
            column = block[:, at : at + 1]
            pivot = block[j : j + 1, :] * (1.0 / column[j : j + 1, :])
            block = jnp.where(sub == j, pivot, block - column * pivot)
        columns = system[:, start : start + 8]
        after = None
        if start + 8 < members:
            after = system[start + 8 : start + 16, low:width]
            terms = [columns[start + 8 : start + 16, j : j + 1] * block[j : j + 1, :] for j in range(8)]
            after = after - (
                ((terms[0] + terms[1]) + (terms[2] + terms[3]))
                + ((terms[4] + terms[5]) + (terms[6] + terms[7]))
            )
            after = after[:, (start + 8) // LANES * LANES - low :]
        outside = (row_number < start) | (row_number >= start + 8)
        columns = jnp.where(outside, columns, 0.0)
        system[:, low:width] = system[:, low:width] - jnp.dot(
            columns, block, preferred_element_type=jnp.float32, precision=lax.Precision.HIGHEST
        )
        system[start : start + 8, low:width] = block
        block = after
    solved = system[:, wide : wide + members]
    weights_ref[...] = solved
    centred = (solved - jnp.sum(solved, axis=0, keepdims=True) / members) / math.sqrt(members - 1)
    turned = centred.T
    high = turned.astype(jnp.bfloat16)
    low_part = (turned - high.astype(jnp.float32)).astype(jnp.bfloat16)
    stores = []
    for n in range(tiles):
        here = slice(n * tile, (n + 1) * tile)
        fetches[n].wait()
        state = slab[:, here]
        moved = jnp.dot(high, state, preferred_element_type=jnp.float32)
        moved = moved + jnp.dot(low_part, state, preferred_element_type=jnp.float32)
        slab[:, here] = (state.astype(jnp.float32) + moved).astype(jnp.bfloat16)
        store = pltpu.make_async_copy(slab.at[:, here], updated_ref.at[:, here], writes.at[n])
        store.start()
        stores.append(store)
    for store in stores:
        store.wait()


def solve(predicted, data, slab, weight_scale):
    pieces = predicted.shape[0]
    members, here = slab.shape
    cells = pieces * LANES
    tiles = 12
    return pl.pallas_call(
        functools.partial(solve_kernel, weight_scale),
        out_shape=(
            jax.ShapeDtypeStruct(slab.shape, jnp.bfloat16),
            jax.ShapeDtypeStruct((members, members), jnp.float32),
            jax.ShapeDtypeStruct((data.shape[0], data.shape[2]), jnp.float32),
        ),
        in_specs=[pl.BlockSpec(memory_space=VMEM)] * 2 + [pl.BlockSpec(memory_space=pltpu.HBM)],
        out_specs=(
            pl.BlockSpec(memory_space=pltpu.HBM),
            pl.BlockSpec(memory_space=VMEM),
            pl.BlockSpec(memory_space=VMEM),
        ),
        scratch_shapes=[
            VMEM((members, cells), jnp.float32),
            VMEM((256 + members, cells), jnp.float32),
            VMEM((members, 512), jnp.float32),
            VMEM((members, here), jnp.bfloat16),
            pltpu.SemaphoreType.DMA((tiles,)),
            pltpu.SemaphoreType.DMA((tiles,)),
        ],
        compiler_params=pltpu.CompilerParams(vmem_limit_bytes=58 * 2**20),
        name="solve",
    )(predicted, data, slab)


def body_small(amplitude_maps, kept_blocks, block_owner, observed, error_scale, perturbation, model_slab):
    members, rows_here, map_width = amplitude_maps.shape
    devices = lax.axis_size("map")
    me = lax.axis_index("map")
    map_height = rows_here * devices
    keep_count = kept_blocks.shape[0]
    columns_here = map_width // devices
    per_column = map_height // BLK
    table_w = jnp.asarray(dct_constant(map_width))
    table_h = jnp.asarray(dct_constant(map_height))

    names = jnp.stack([kept_blocks, block_owner[:, 0]])
    names = jnp.pad(names, ((0, 6), (0, LANES - keep_count)))
    names = gather_names(names, devices)[:, :, :keep_count]
    local = jnp.concatenate(
        [perturbation, observed[:, None], error_scale[:, None]], axis=1
    )
    local = lax.all_gather(local, "map", tiled=True)

    blocks = names[:, 0, :].reshape(-1)
    owners = names[:, 1, :]
    source = jnp.repeat(jnp.arange(devices, dtype=jnp.int32), keep_count)
    column_of = source * columns_here + blocks // per_column
    row_of = blocks % per_column
    one = jnp.bfloat16
    pick_column = (column_of[:, None] == jnp.arange(map_width, dtype=jnp.int32)[None, :]).astype(one)
    row_table = jnp.dot(pick_column, table_w, preferred_element_type=jnp.float32).astype(one)
    pick_row = (row_of[:, None] == jnp.arange(per_column, dtype=jnp.int32)[None, :]).astype(one)
    here = lax.dynamic_slice_in_dim(table_h, me * rows_here, rows_here, axis=1)
    column_table = jnp.einsum(
        "bk,kch->hcb",
        pick_row,
        here.reshape(per_column, BLK, rows_here),
        preferred_element_type=jnp.float32,
    )
    parts = transform(amplitude_maps, row_table, column_table)
    predicted = combine(parts)

    positions = jnp.arange(keep_count, dtype=jnp.int32)
    earlier = (owners[:, :, None] == owners[:, None, :]) & (
        positions[None, None, :] < positions[None, :, None]
    )
    rank = jnp.sum(earlier.astype(jnp.int32), axis=2)
    slot = ((owners * devices + jnp.arange(devices, dtype=jnp.int32)[:, None]) * CAP + rank).reshape(-1)
    slots = devices * devices * CAP
    pick_slot = (jnp.arange(slots, dtype=jnp.int32)[:, None] == slot[None, :]).astype(one)
    data = jnp.einsum(
        "sce,sb->ceb",
        local.reshape(slots, BLK, members + 2),
        pick_slot,
        preferred_element_type=jnp.float32,
    ).astype(one)
    weight_scale = members / (devices * keep_count * BLK)
    updated_slab, update_weights, misfit = solve(predicted, data, model_slab, weight_scale)
    mine = lax.dynamic_slice_in_dim(pick_slot, me * devices * CAP, devices * CAP, axis=0)
    data_misfit = jnp.einsum(
        "sb,cb->sc", mine.astype(jnp.float32), misfit, precision=lax.Precision.HIGHEST
    ).reshape(-1)
    return (updated_slab, update_weights, data_misfit)


def solution(mesh):
    in_specs = (
        P("groups", "map", None),
        P(("groups", "map")),
        P(("groups", "map"), None),
        P(("groups", "map")),
        P(("groups", "map")),
        P(("groups", "map"), None),
        P(None, ("groups", "map")),
    )
    out_specs = (P(None, ("groups", "map")), P("groups", None), P(("groups", "map")))
    devices = mesh.shape["map"]

    def run(*args):
        kept = args[1].shape[0] // mesh.shape["groups"]
        fits = devices == 16 and kept * BLK == devices * LANES
        body = body_small if fits else body_large
        return jax.shard_map(body, mesh=mesh, in_specs=in_specs, out_specs=out_specs, check_vma=False)(*args)

    return run
```

```python
import functools
import math

import jax
import jax.numpy as jnp
import numpy as np
from jax import lax
from jax.experimental import pallas as pl
from jax.experimental.pallas import tpu as pltpu
from jax.sharding import PartitionSpec as P

BLK = 8
CAP = 2
LANES = 128


inflation = 4.0
epsilon = 1e-06
MESH = pl.DeviceIdType.MESH
VMEM = pltpu.VMEM


def dct_table(length):
    frequency = jnp.arange(length, dtype=jnp.float32)[:, None]
    sample = jnp.arange(length, dtype=jnp.float32)[None, :]
    cosine_table = jnp.cos(math.pi * (2.0 * sample + 1.0) * frequency / (2.0 * length))
    factor = jnp.where(frequency == 0, math.sqrt(1.0 / length), math.sqrt(2.0 / length))
    return (cosine_table * factor).astype(jnp.bfloat16)


def dct_constant(length):
    f32 = np.float32
    frequency = np.arange(length, dtype=f32)[:, None]
    sample = np.arange(length, dtype=f32)[None, :]
    angle = f32(math.pi) * (f32(2) * sample + f32(1)) * frequency / f32(2 * length)
    cosine_table = np.cos(angle.astype(np.float64)).astype(f32)
    factor = np.where(frequency == 0, f32(math.sqrt(1.0 / length)), f32(math.sqrt(2.0 / length)))
    return (cosine_table * factor).astype(jnp.bfloat16)


def gram_terms(predicted, observed_rows, scale_rows, noise_rows, live_mask, weight_scale):
    members = predicted.shape[1]
    center = jnp.mean(predicted, axis=1, keepdims=True)
    anomaly = (predicted - center) / math.sqrt(members - 1)
    weight = live_mask * weight_scale / (scale_rows * scale_rows)
    mismatch = (
        observed_rows[:, None] + math.sqrt(inflation) * scale_rows[:, None] * noise_rows - predicted
    )
    weighted = anomaly * weight[:, None]
    contract = (((0,), (0,)), ((), ()))
    gram_matrix = lax.dot_general(anomaly, weighted, contract, precision=lax.Precision.HIGHEST)
    cross_terms = lax.dot_general(weighted, mismatch, contract, precision=lax.Precision.HIGHEST)
    relative = mismatch / scale_rows[:, None]
    misfit_rows = live_mask * jnp.sqrt(jnp.mean(relative * relative, axis=1) + epsilon)
    return (gram_matrix, cross_terms, misfit_rows)


def solve_weights(gram_matrix, cross_terms):
    members = gram_matrix.shape[0]
    factor = jnp.linalg.cholesky(gram_matrix + inflation * jnp.eye(members, dtype=jnp.float32))
    return jax.scipy.linalg.cho_solve((factor, True), cross_terms)


def update_state(block, update_weights):
    state = block.astype(jnp.float32)
    members = state.shape[0]
    anomaly = (state - jnp.mean(state, axis=0, keepdims=True)) / math.sqrt(members - 1)
    moved = state + lax.dot_general(
        update_weights, anomaly, (((0,), (0,)), ((), ())), precision=lax.Precision.HIGHEST
    )
    return moved.astype(jnp.bfloat16)


def body_large(amplitude_maps, kept_blocks, block_owner, observed, error_scale, perturbation, model_slab):
    members, rows_here, map_width = amplitude_maps.shape
    devices = lax.axis_size("map")
    map_height = rows_here * devices
    table_w = dct_table(map_width)
    table_h = dct_table(map_height)
    rowwise = jnp.einsum(
        "ehw,kw->hke", amplitude_maps, table_w, preferred_element_type=jnp.float32
    ).astype(jnp.bfloat16)
    coefficients = jnp.einsum(
        "kh,hwe->wke",
        table_h,
        lax.all_to_all(rowwise, "map", split_axis=1, concat_axis=0, tiled=True),
        preferred_element_type=jnp.float32,
    ).astype(jnp.bfloat16)
    block_rows = coefficients.reshape(-1, BLK * members)
    candidates = block_rows.shape[0]
    keep_count = kept_blocks.shape[0]
    slot_count = devices * CAP
    dest_owner = block_owner[:, 0]
    positions = jnp.arange(keep_count, dtype=jnp.int32)
    earlier = (dest_owner[:, None] == dest_owner[None, :]) & (
        positions[None, :] < positions[:, None]
    )
    slot_rank = jnp.sum(earlier.astype(jnp.int32), axis=1)
    slot_index = dest_owner * CAP + slot_rank
    pick_slot = (slot_index[:, None] == jnp.arange(slot_count, dtype=jnp.int32)[None, :]).astype(
        jnp.bfloat16
    )
    weight_scale = members / (devices * keep_count * BLK)
    contract = (((0,), (0,)), ((), ()))
    pick_block = (kept_blocks[:, None] == jnp.arange(candidates, dtype=jnp.int32)[None, :]).astype(
        jnp.bfloat16
    )
    routing = lax.dot_general(
        pick_slot, pick_block, contract, preferred_element_type=jnp.float32
    ).astype(jnp.bfloat16)
    outgoing = jnp.dot(routing, block_rows, preferred_element_type=jnp.float32).astype(jnp.bfloat16)
    live_slots = jnp.sum(pick_slot.astype(jnp.float32), axis=0).astype(jnp.bfloat16)
    arrived, arrived_live = (
        lax.all_to_all(
            outgoing.reshape(devices, CAP, BLK * members),
            "map",
            split_axis=0,
            concat_axis=0,
            tiled=True,
        ),
        lax.all_to_all(
            live_slots.reshape(devices, CAP), "map", split_axis=0, concat_axis=0, tiled=True
        ),
    )
    predicted = arrived.reshape(-1, members).astype(jnp.float32)
    live_mask = jnp.repeat(arrived_live.astype(jnp.float32).reshape(-1), BLK)
    gram_matrix, cross_terms, data_misfit = gram_terms(
        predicted,
        observed.astype(jnp.float32),
        error_scale.astype(jnp.float32),
        perturbation.astype(jnp.float32),
        live_mask,
        weight_scale,
    )
    gram_matrix, cross_terms = lax.psum((gram_matrix, cross_terms), "map")
    update_weights = solve_weights(gram_matrix, cross_terms)
    updated_slab = update_state(model_slab, update_weights)
    return (updated_slab, update_weights, data_misfit)


def transform_kernel(rows_here, maps_ref, row_table_ref, column_table_ref, part_ref, rowwise_ref):
    chunk, _, width = maps_ref.shape
    flat = maps_ref[...].reshape(chunk * rows_here, width)
    rowwise = lax.dot_general(
        flat, row_table_ref[...], (((1,), (1,)), ((), ())), preferred_element_type=jnp.float32
    )
    halves = rowwise_ref.shape[0]
    for half in range(halves):
        rowwise_ref[half] = rowwise[:, half * LANES : (half + 1) * LANES]

    tiles = range(chunk // 8)
    for half in range(halves):
        lanes = slice(half * LANES, (half + 1) * LANES)
        total = [[None] * BLK for _ in tiles]
        for h in range(rows_here):
            rows = []
            for t in tiles:
                row = rowwise_ref[half, pl.ds(t * 8 * rows_here + h, 8, stride=rows_here), :]
                rows.append(row.astype(jnp.bfloat16).astype(jnp.float32))
            for c in range(BLK):
                entry = column_table_ref[h, c : c + 1, lanes]
                for t in tiles:
                    term = rows[t] * entry
                    total[t][c] = term if h == 0 else total[t][c] + term
        for t in tiles:
            for c in range(BLK):
                part_ref[c * halves + half, t * 8 : t * 8 + 8, :] = total[t][c]


def transform(maps, row_table, column_table):
    members, rows_here, width = maps.shape
    blocks = row_table.shape[0]
    chunk = 40
    pieces = BLK * blocks // LANES
    return pl.pallas_call(
        functools.partial(transform_kernel, rows_here),
        grid=(members // chunk,),
        out_shape=jax.ShapeDtypeStruct((pieces, members, LANES), jnp.float32),
        in_specs=[
            pl.BlockSpec((chunk, rows_here, width), lambda i: (i, 0, 0)),
            pl.BlockSpec((blocks, width), lambda i: (0, 0)),
            pl.BlockSpec((rows_here, BLK, blocks), lambda i: (0, 0, 0)),
        ],
        out_specs=pl.BlockSpec((pieces, chunk, LANES), lambda i: (0, i, 0)),
        scratch_shapes=[VMEM((blocks // LANES, chunk * rows_here, LANES), jnp.float32)],
        compiler_params=pltpu.CompilerParams(vmem_limit_bytes=58 * 2**20),
        name="transform",
    )(maps, row_table, column_table)


def names_kernel(names_ref, all_ref, sends, recvs):
    devices = all_ref.shape[0]
    me = lax.axis_index("map")
    peers = [lax.rem(me + s, devices) for s in range(1, devices)]
    barrier = pltpu.get_barrier_semaphore()
    for peer in peers:
        pl.semaphore_signal(barrier, inc=1, device_id={"map": peer}, device_id_type=MESH)
    pl.semaphore_wait(barrier, devices - 1)
    copies = []
    for s, peer in enumerate(peers):
        copy = pltpu.make_async_remote_copy(
            src_ref=names_ref,
            dst_ref=all_ref.at[me],
            send_sem=sends.at[s],
            recv_sem=recvs.at[s],
            device_id={"map": peer},
            device_id_type=MESH,
        )
        copy.start()
        copies.append(copy)
    all_ref[me] = names_ref[...]
    for copy in copies:
        copy.wait()


def gather_names(names, devices):
    return pl.pallas_call(
        names_kernel,
        out_shape=jax.ShapeDtypeStruct((devices,) + names.shape, names.dtype),
        in_specs=[pl.BlockSpec(memory_space=VMEM)],
        out_specs=pl.BlockSpec(memory_space=VMEM),
        scratch_shapes=[
            pltpu.SemaphoreType.DMA((devices - 1,)),
            pltpu.SemaphoreType.DMA((devices - 1,)),
        ],
        compiler_params=pltpu.CompilerParams(collective_id=1, has_side_effects=True),
        name="names",
    )(names)


def combine_kernel(
    part_ref, out_ref, held, from_core, from_x, from_z, sends, recvs
):
    members = part_ref.shape[1]
    me = lax.axis_index("map")
    core = lax.rem(me, 2)
    x = lax.rem(me // 2, 2)
    z = me // 4
    core_peer = me + 1 - 2 * core
    x_peer = me + 2 - 4 * x
    z_peers = [lax.rem(z + s, 4) * 4 + x * 2 + core for s in (1, 2, 3)]

    barrier = pltpu.get_barrier_semaphore()
    for peer in [core_peer, x_peer] + z_peers:
        pl.semaphore_signal(barrier, inc=1, device_id={"map": peer}, device_id_type=MESH)
    pl.semaphore_wait(barrier, 5)

    def send(number, src, dst, peer):
        copy = pltpu.make_async_remote_copy(
            src_ref=src,
            dst_ref=dst,
            send_sem=sends.at[number],
            recv_sem=recvs.at[number],
            device_id={"map": peer},
            device_id_type=MESH,
        )
        copy.start()
        return copy

    order = (2, 1, 3, 0)
    zs = [lax.rem(z + s, 4) for s in order]
    first = []
    for n in range(8):
        xx = 1 - x if n < 4 else x
        piece = zs[n % 4] * 4 + xx * 2 + 1 - core
        first.append(send(n, part_ref.at[piece], from_core.at[n], core_peer))
    second = []
    for n in range(4):
        first[n].wait_recv()
        held[n] = part_ref[zs[n] * 4 + (1 - x) * 2 + core] + from_core[n]
        second.append(send(8 + n, held.at[n], from_x.at[n], x_peer))
    third = []
    for n, s in enumerate(order):
        first[4 + n].wait_recv()
        own = part_ref[zs[n] * 4 + x * 2 + core] + from_core[4 + n]
        second[n].wait_recv()
        held[4 + n] = own + from_x[n]
        if s:
            third.append(send(12 + n, held.at[4 + n], from_z.at[n], z_peers[s - 1]))
    for copy in third:
        copy.wait_recv()
    total = held[7] + from_z[0] + from_z[1] + from_z[2]
    pad = out_ref.shape[1] - members
    mine = jnp.concatenate([total, jnp.zeros((pad, LANES), jnp.float32)], axis=0)
    out_ref[me] = mine.astype(jnp.bfloat16)

    fourth = [send(15 + s, out_ref.at[me], out_ref.at[me], z_peers[s]) for s in range(3)]
    fifth = [send(18, out_ref.at[me], out_ref.at[me], x_peer)]
    sixth = [send(22, out_ref.at[me], out_ref.at[me], core_peer)]
    for s in range(3):
        fourth[s].wait_recv()
        piece = lax.rem(z + 3 - s, 4) * 4 + x * 2 + core
        fifth.append(send(19 + s, out_ref.at[piece], out_ref.at[piece], x_peer))
        sixth.append(send(23 + s, out_ref.at[piece], out_ref.at[piece], core_peer))
    for n in range(4):
        fifth[n].wait_recv()
        piece = lax.rem(z + 4 - n, 4) * 4 + (1 - x) * 2 + core
        sixth.append(send(26 + n, out_ref.at[piece], out_ref.at[piece], core_peer))
    for copy in sixth:
        copy.wait_recv()
    for copy in first + second + third + fourth + fifth + sixth:
        copy.wait_send()


def combine(parts):
    pieces, members, _ = parts.shape
    padded = -(-members // 16) * 16
    piece = (members, LANES)
    return pl.pallas_call(
        combine_kernel,
        out_shape=jax.ShapeDtypeStruct((pieces, padded, LANES), jnp.bfloat16),
        in_specs=[pl.BlockSpec(memory_space=VMEM)],
        out_specs=pl.BlockSpec(memory_space=VMEM),
        scratch_shapes=[
            VMEM((8,) + piece, jnp.float32),
            VMEM((8,) + piece, jnp.float32),
            VMEM((4,) + piece, jnp.float32),
            VMEM((3,) + piece, jnp.float32),
            pltpu.SemaphoreType.DMA((30,)),
            pltpu.SemaphoreType.DMA((30,)),
        ],
        compiler_params=pltpu.CompilerParams(
            collective_id=0, has_side_effects=True, vmem_limit_bytes=40 * 2**20
        ),
        name="combine",
    )(parts)


def solve_kernel(
    weight_scale, predicted_ref, data_ref, slab_ref, updated_ref, weights_ref, misfit_ref,
    weighted, paired, system, slab, reads, writes,
):
    pieces = predicted_ref.shape[0]
    members = weights_ref.shape[0]
    halves = data_ref.shape[2] // LANES
    wide = 256
    tiles = reads.shape[0]
    tile = slab.shape[1] // tiles
    fetches = []
    for n in range(tiles):
        here = slice(n * tile, (n + 1) * tile)
        fetch = pltpu.make_async_copy(slab_ref.at[:, here], slab.at[:, here], reads.at[n])
        fetch.start()
        fetches.append(fetch)
    for n in range(pieces):
        c, half = divmod(n, halves)
        lanes = slice(half * LANES, (half + 1) * LANES)
        here = slice(n * LANES, (n + 1) * LANES)
        predicted = predicted_ref[n].astype(jnp.float32)[:members]
        data = data_ref[c, :, lanes].astype(jnp.float32)
        noise = data[:members]
        observed = data[members : members + 1]
        scale = data[members + 1 : members + 2]
        center = jnp.sum(predicted, axis=0, keepdims=True) / members
        anomaly = (predicted - center) * (1.0 / math.sqrt(members - 1))
        weight = weight_scale / (scale * scale)
        mismatch = observed + math.sqrt(inflation) * scale * noise - predicted
        squares = jnp.sum(mismatch * mismatch, axis=0, keepdims=True) / (scale * scale)
        misfit_ref[c : c + 1, lanes] = jnp.sqrt(squares / members + epsilon)
        weighted[:, here] = anomaly * weight
        paired[0:members, here] = anomaly
        paired[wide : wide + members, here] = mismatch
    paired[members:wide, :] = jnp.zeros((wide - members, paired.shape[1]), jnp.float32)
    product = lax.dot_general(
        weighted[...], paired[...], (((1,), (1,)), ((), ())),
        preferred_element_type=jnp.float32, precision=lax.Precision.HIGHEST,
    )
    i = lax.broadcasted_iota(jnp.int32, product.shape, 0)
    j = lax.broadcasted_iota(jnp.int32, product.shape, 1)
    system[:, 0 : wide + members] = product + jnp.where(i == j, inflation, 0.0)
    width = system.shape[1]
    size = 16
    row_number = lax.broadcasted_iota(jnp.int32, (members, 1), 0)
    block = system[0:size, :]
    for start in range(0, members, size):
        low = start // LANES * LANES
        stop = min(start + size, members)
        sub = lax.broadcasted_iota(jnp.int32, (stop - start, 1), 0)
        for j in range(stop - start):
            at = start - low + j
            column = block[:, at : at + 1]
            pivot = block[j : j + 1, :] * (1.0 / column[j : j + 1, :])
            block = jnp.where(sub == j, pivot, block - column * pivot)
        columns = system[:, start:stop]
        after = None
        if stop < members:
            end = min(stop + size, members)
            after = system[stop:end, low:width]
            terms = [columns[stop:end, j : j + 1] * block[j : j + 1, :] for j in range(stop - start)]
            while len(terms) > 1:
                terms = [terms[n] + terms[n + 1] for n in range(0, len(terms), 2)]
            after = (after - terms[0])[:, stop // LANES * LANES - low :]
        outside = (row_number < start) | (row_number >= stop)
        columns = jnp.where(outside, columns, 0.0)
        system[:, low:width] = system[:, low:width] - jnp.dot(
            columns, block, preferred_element_type=jnp.float32, precision=lax.Precision.HIGHEST
        )
        system[start:stop, low:width] = block
        block = after
    solved = system[:, wide : wide + members]
    weights_ref[...] = solved
    centred = (solved - jnp.sum(solved, axis=0, keepdims=True) / members) / math.sqrt(members - 1)
    turned = centred.T
    high = turned.astype(jnp.bfloat16)
    low_part = (turned - high.astype(jnp.float32)).astype(jnp.bfloat16)
    stores = []
    for n in range(tiles):
        here = slice(n * tile, (n + 1) * tile)
        fetches[n].wait()
        state = slab[:, here]
        moved = jnp.dot(high, state, preferred_element_type=jnp.float32)
        moved = moved + jnp.dot(low_part, state, preferred_element_type=jnp.float32)
        slab[:, here] = (state.astype(jnp.float32) + moved).astype(jnp.bfloat16)
        store = pltpu.make_async_copy(slab.at[:, here], updated_ref.at[:, here], writes.at[n])
        store.start()
        stores.append(store)
    for store in stores:
        store.wait()


def solve(predicted, data, slab, weight_scale):
    pieces = predicted.shape[0]
    members, here = slab.shape
    cells = pieces * LANES
    tiles = 12
    return pl.pallas_call(
        functools.partial(solve_kernel, weight_scale),
        out_shape=(
            jax.ShapeDtypeStruct(slab.shape, jnp.bfloat16),
            jax.ShapeDtypeStruct((members, members), jnp.float32),
            jax.ShapeDtypeStruct((data.shape[0], data.shape[2]), jnp.float32),
        ),
        in_specs=[pl.BlockSpec(memory_space=VMEM)] * 2 + [pl.BlockSpec(memory_space=pltpu.HBM)],
        out_specs=(
            pl.BlockSpec(memory_space=pltpu.HBM),
            pl.BlockSpec(memory_space=VMEM),
            pl.BlockSpec(memory_space=VMEM),
        ),
        scratch_shapes=[
            VMEM((members, cells), jnp.float32),
            VMEM((256 + members, cells), jnp.float32),
            VMEM((members, 512), jnp.float32),
            VMEM((members, here), jnp.bfloat16),
            pltpu.SemaphoreType.DMA((tiles,)),
            pltpu.SemaphoreType.DMA((tiles,)),
        ],
        compiler_params=pltpu.CompilerParams(vmem_limit_bytes=58 * 2**20),
        name="solve",
    )(predicted, data, slab)


def body_small(amplitude_maps, kept_blocks, block_owner, observed, error_scale, perturbation, model_slab):
    members, rows_here, map_width = amplitude_maps.shape
    devices = lax.axis_size("map")
    me = lax.axis_index("map")
    map_height = rows_here * devices
    keep_count = kept_blocks.shape[0]
    columns_here = map_width // devices
    per_column = map_height // BLK
    table_w = jnp.asarray(dct_constant(map_width))
    table_h = jnp.asarray(dct_constant(map_height))

    names = jnp.stack([kept_blocks, block_owner[:, 0]])
    names = jnp.pad(names, ((0, 6), (0, LANES - keep_count)))
    names = gather_names(names, devices)[:, :, :keep_count]
    local = jnp.concatenate(
        [perturbation, observed[:, None], error_scale[:, None]], axis=1
    )
    local = lax.all_gather(local, "map", tiled=True)

    blocks = names[:, 0, :].reshape(-1)
    owners = names[:, 1, :]
    source = jnp.repeat(jnp.arange(devices, dtype=jnp.int32), keep_count)
    column_of = source * columns_here + blocks // per_column
    row_of = blocks % per_column
    one = jnp.bfloat16
    pick_column = (column_of[:, None] == jnp.arange(map_width, dtype=jnp.int32)[None, :]).astype(one)
    row_table = jnp.dot(pick_column, table_w, preferred_element_type=jnp.float32).astype(one)
    pick_row = (row_of[:, None] == jnp.arange(per_column, dtype=jnp.int32)[None, :]).astype(one)
    here = lax.dynamic_slice_in_dim(table_h, me * rows_here, rows_here, axis=1)
    column_table = jnp.einsum(
        "bk,kch->hcb",
        pick_row,
        here.reshape(per_column, BLK, rows_here),
        preferred_element_type=jnp.float32,
    )
    parts = transform(amplitude_maps, row_table, column_table)
    predicted = combine(parts)

    positions = jnp.arange(keep_count, dtype=jnp.int32)
    earlier = (owners[:, :, None] == owners[:, None, :]) & (
        positions[None, None, :] < positions[None, :, None]
    )
    rank = jnp.sum(earlier.astype(jnp.int32), axis=2)
    slot = ((owners * devices + jnp.arange(devices, dtype=jnp.int32)[:, None]) * CAP + rank).reshape(-1)
    slots = devices * devices * CAP
    pick_slot = (jnp.arange(slots, dtype=jnp.int32)[:, None] == slot[None, :]).astype(one)
    data = jnp.einsum(
        "sce,sb->ceb",
        local.reshape(slots, BLK, members + 2),
        pick_slot,
        preferred_element_type=jnp.float32,
    ).astype(one)
    weight_scale = members / (devices * keep_count * BLK)
    updated_slab, update_weights, misfit = solve(predicted, data, model_slab, weight_scale)
    mine = lax.dynamic_slice_in_dim(pick_slot, me * devices * CAP, devices * CAP, axis=0)
    data_misfit = jnp.einsum(
        "sb,cb->sc", mine.astype(jnp.float32), misfit, precision=lax.Precision.HIGHEST
    ).reshape(-1)
    return (updated_slab, update_weights, data_misfit)


def solution(mesh):
    in_specs = (
        P("groups", "map", None),
        P(("groups", "map")),
        P(("groups", "map"), None),
        P(("groups", "map")),
        P(("groups", "map")),
        P(("groups", "map"), None),
        P(None, ("groups", "map")),
    )
    out_specs = (P(None, ("groups", "map")), P("groups", None), P(("groups", "map")))
    devices = mesh.shape["map"]

    def run(*args):
        kept = args[1].shape[0] // mesh.shape["groups"]
        fits = devices == 16 and kept * BLK == devices * LANES
        body = body_small if fits else body_large
        return jax.shard_map(body, mesh=mesh, in_specs=in_specs, out_specs=out_specs, check_vma=False)(*args)

    return run
```
